32 devices in a mesh: groups: 2 (over x), head: 8 (over z, y), dp: 2 (over core).
Axes of the slice: x: 2, y: 2, z: 4, core: 2. Of those that a mesh axis runs over, the one named last changes fastest.
Arguments:
- head_outputs: bfloat16 [768, 8, 128], P(('groups', 'head', 'dp')), parts along dimension 0, may hold values from -91 to 91
- active: int32 [768, 8, 32], P(('groups', 'head', 'dp')), parts along dimension 0, may hold values from 0 to 8191, as said below
- enc_weight: bfloat16 [16, 8192, 128], P(('groups', 'head')), parts along dimension 0, may hold values from -0.5 to 0.5
- enc_bias: float32 [16, 8192], P(('groups', 'head')), parts along dimension 0, may hold values from -3 to 3
- dec_weight: bfloat16 [16, 8192, 128], P(('groups', 'head')), parts along dimension 0, may hold values from -1 to 1
- dec_bias: float32 [16, 128], P(('groups', 'head')), parts along dimension 0, may hold values from -3 to 3
Outputs:
- reconstruction: bfloat16 [768, 8, 128], P(('groups', 'head', 'dp')), parts along dimension 0
- explained: float32 [16], P(('groups', 'head')), parts along dimension 0
- dec_gradient: float32 [16, 8192, 128], P(('groups', 'head'), 'dp'), parts along dimension 0
The draws below stay inside these ranges and needn't reach their ends.
There are 2 independent parts, one for each index of `groups`. The reference program is written for one: setup_inputs(seed, part) draws one part's arguments, and reference() takes and returns one part's arrays. A program takes and returns all parts, laid end to end along the dimension named above; each array names one. Nothing has to cross between parts.
Inputs may be any that keep to these rules, and one draw needn't show every extreme that they name: `active`: the 32 indices of one token and head lie one in each block of 256 consecutive latents, so they are distinct.
All inputs are finite; a program needn't handle non-finite values.
Results may differ from the reference program's by a relative error of at most 0.0069.
Values may be sent and summed in bfloat16 or wider, within the bound.
A program may use at most 64 MiB of HBM per device.

```python
import math
import jax
import jax.numpy as jnp
from jax import lax

D = 128
LAT = 8192
TOP = 32
TOK_DEV = 24
HEADS = 8
TOKENS = 384
N_DP = 2


def draw_head_outputs(key, part):
    key = jax.random.fold_in(key, 17)
    key_base, key_rough, key_head = jax.random.split(key, 3)
    position = jnp.arange(TOKENS, dtype=jnp.float32) / TOKENS
    rising = jnp.power(3.0, position)[:, None, None]
    rough = jnp.exp(jax.random.uniform(key_rough, (TOKENS, 1, 1), jnp.float32, -0.7, 0.7))
    head_scale = jnp.exp(jax.random.uniform(key_head, (1, HEADS, 1), jnp.float32, math.log(0.3), math.log(3.0)))
    base = jnp.clip(jax.random.normal(key_base, (TOKENS, HEADS, D), jnp.float32), -5.0, 5.0)
    return (base * rising * rough * head_scale).astype(jnp.bfloat16)


def draw_active(key, part):
    key = jax.random.fold_in(key, 29)
    key_offset, key_turn = jax.random.split(key, 2)
    stride = LAT // TOP
    offsets = jax.random.randint(key_offset, (TOKENS, HEADS, TOP), 0, stride, jnp.int32)
    turns = jax.random.randint(key_turn, (TOKENS, HEADS, 1), 0, TOP, jnp.int32)
    turns = turns.at[0, 0, 0].set(0)
    bands = (jnp.arange(TOP, dtype=jnp.int32)[None, None, :] + turns) % TOP
    indices = bands * stride + offsets
    indices = indices.at[0, 0, 0].set(0)
    indices = indices.at[0, 0, TOP - 1].set(LAT - 1)
    return indices.astype(jnp.int32)


def levels(own_key, shape, shards, smallest, largest):
    level = 1.0
    for dim, blocks in shards:
        heights = jax.random.uniform(jax.random.fold_in(jax.random.fold_in(own_key, 6), dim), (blocks,), jnp.float32, smallest / len(shards), largest / len(shards))
        level = level * jnp.repeat(jnp.exp(heights), shape[dim] // blocks).reshape((-1,) + (1,) * (len(shape) - 1 - dim))
    return level


def bell_draw(rng, extent, width, reach, cuts=(), kind=jnp.bfloat16):
    result = jax.random.normal(rng, extent, jnp.float32) * width
    if len(cuts) > 0:
        result = levels(rng, extent, cuts, -0.22, 0.18) * result
    return jnp.clip(result, min=-reach, max=reach).astype(kind)


def setup_inputs(seed: int = 0, part: int = 0) -> dict:
    keys = jax.random.split(jax.random.key(seed), 7)
    part_keys = jax.random.split(jax.random.fold_in(keys[6], part), 7)
    return {
        "head_outputs": draw_head_outputs(jax.random.fold_in(jax.random.fold_in(keys[6], part), 71), part),
        "active": draw_active(jax.random.fold_in(jax.random.fold_in(keys[6], part), 71), part),
        "enc_weight": bell_draw(part_keys[2], (HEADS, LAT, D), D ** -0.5, 0.5, ((0, 8),)),
        "enc_bias": bell_draw(part_keys[3], (HEADS, LAT), 0.5, 3.0, ((0, 8),), jnp.float32),
        "dec_weight": bell_draw(part_keys[4], (HEADS, LAT, D), TOP ** -0.5, 1.0, ((0, 8),)),
        "dec_bias": bell_draw(part_keys[5], (HEADS, D), 0.5, 3.0, ((0, 8),), jnp.float32),
    }


EPSILON = 1e-06

def reference(head_outputs, active, enc_weight, enc_bias, dec_weight, dec_bias):
    as_float = head_outputs.astype(jnp.float32)
    squares = lax.optimization_barrier(jnp.sum(as_float * as_float, axis=(0, 2)))
    sum_rows = lax.optimization_barrier(jnp.sum(as_float, axis=0))
    norm_scale = lax.rsqrt(squares / (TOKENS * D) + EPSILON)
    center = sum_rows * norm_scale[:, None] / TOKENS
    factor = LAT / (TOKENS * TOP)
    halves = jnp.arange(TOKENS) // TOK_DEV % N_DP

    def one_head(inputs):
        rows, picked, enc_mat, enc_vec, dec_mat, dec_vec, head_scale, head_center = inputs
        normed = rows.astype(jnp.float32) * head_scale
        encoder_in = (normed - dec_vec).astype(jnp.bfloat16)
        enc_rows = jnp.take(enc_mat, picked, axis=0).astype(jnp.float32)
        latent_codes = jnp.einsum('rd,rkd->rk', encoder_in.astype(jnp.float32), enc_rows)
        latent_codes = (latent_codes + jnp.take(enc_vec, picked, axis=0)).astype(jnp.bfloat16)
        dec_rows = jnp.take(dec_mat, picked, axis=0).astype(jnp.float32)
        recon_normed = jnp.einsum('rk,rkd->rd', latent_codes.astype(jnp.float32), dec_rows) + dec_vec
        rebuilt = (recon_normed / head_scale).astype(jnp.bfloat16)
        mismatch = recon_normed - normed
        scaled_error = (mismatch * factor).astype(jnp.bfloat16)
        products = latent_codes.astype(jnp.float32)[:, :, None] * scaled_error.astype(jnp.float32)[:, None, :]
        gradient = jnp.zeros((LAT, D), jnp.float32)
        for shard in range(N_DP):
            keep = (halves == shard).astype(jnp.float32)[:, None, None]
            block_term = jnp.zeros((LAT, D), jnp.float32).at[picked].add(products * keep)
            gradient = gradient + lax.optimization_barrier(block_term.astype(jnp.bfloat16)).astype(jnp.float32)
        error_sum = jnp.sum(mismatch * mismatch)
        spread_sum = jnp.sum(jnp.square(normed - head_center))
        return (rebuilt, 1.0 - error_sum / spread_sum, gradient)
    rebuilt, explained, dec_gradient = lax.map(one_head, (jnp.transpose(head_outputs, (1, 0, 2)), jnp.transpose(active, (1, 0, 2)), enc_weight, enc_bias, dec_weight, dec_bias, norm_scale, center))
    return (jnp.transpose(rebuilt, (1, 0, 2)), explained, dec_gradient)
```

```python
import functools

import jax
import jax.numpy as jnp
from jax import lax
from jax.experimental import pallas as pl
from jax.experimental.pallas import tpu as pltpu
from jax.sharding import PartitionSpec as P

EPSILON = 1e-06
F32 = jnp.float32
BF16 = jnp.bfloat16
MESH = pl.DeviceIdType.MESH
PAD = 16


def round_up(value, unit):
    return (value + unit - 1) // unit * unit


def step_kernel(
    heads, shards, x_ref, act_ref, encw_ref, encb_ref, decw_ref, decb_ref,
    recon_ref, expl_ref, grad_ref,
    xs, acts, msg, inbox, wide, dec, dec_t, bias, codes, offs, acc, acc_in, rebuilt, reply, back, result,
    local_sem, send_a, recv_a, send_b, recv_b, send_c, recv_c,
):
    tok = x_ref.shape[0]
    feat = x_ref.shape[2]
    top = act_ref.shape[2]
    latents = encw_ref.shape[1]
    share = latents // shards
    stride = latents // top
    shift = stride.bit_length() - 1
    blocks = share // stride
    peers = heads * shards
    rows = peers * tok
    my_h = lax.axis_index("head")
    my_d = lax.axis_index("dp")
    me = my_h * shards + my_d

    first = pl.multiple_of(my_d * share, share)
    load_w = pltpu.make_async_copy(
        encw_ref.at[0, pl.ds(first, share), :], wide.at[:, pl.ds(0, feat)], local_sem.at[0]
    )
    load_d = pltpu.make_async_copy(decw_ref.at[0, pl.ds(first, share), :], dec, local_sem.at[1])
    load_b = pltpu.make_async_copy(encb_ref.at[:, pl.ds(first, share)], bias, local_sem.at[2])
    load_d.start()
    load_b.start()
    load_w.start()

    barrier = pltpu.get_barrier_semaphore()

    def greet(step, carry):
        peer = lax.rem(me + step, peers)
        pl.semaphore_signal(
            barrier, inc=1,
            device_id={"head": peer // shards, "dp": lax.rem(peer, shards)}, device_id_type=MESH,
        )
        return carry

    lax.fori_loop(1, peers, greet, 0)

    xs[...] = x_ref[...].astype(F32).reshape(tok * heads, feat)
    picked = act_ref[...].reshape(tok * heads, top)
    acts[...] = jnp.zeros_like(acts)
    acts[:, 0:top] = (picked & (stride - 1)).astype(F32)
    acts[:, top : 2 * top] = (picked >> shift).astype(F32)
    for h in range(heads):
        both = jnp.concatenate(
            [xs[pl.ds(h, tok, stride=heads), :], acts[pl.ds(h, tok, stride=heads), :]], axis=0
        )
        msg[h] = both.astype(BF16)
    pl.semaphore_wait(barrier, peers - 1)

    def copy_a(peer, slot):
        return pltpu.make_async_remote_copy(
            src_ref=msg.at[peer // shards],
            dst_ref=inbox.at[slot],
            send_sem=send_a.at[peer],
            recv_sem=recv_a.at[slot],
            device_id={"head": peer // shards, "dp": lax.rem(peer, shards)},
            device_id_type=MESH,
        )

    def send_rows(step, carry):
        copy_a(lax.rem(me + step, peers), me).start()
        return carry

    lax.fori_loop(1, peers, send_rows, 0)
    inbox[me] = msg[my_h]

    load_b.wait()
    whole = bias[...]
    high = whole.astype(BF16).astype(F32)
    mid = (whole - high).astype(BF16).astype(F32)
    low = whole - high - mid
    stacked = jnp.concatenate([high, mid, low, jnp.zeros((5, share), F32)], axis=0)
    wide[:, pl.ds(feat, feat)] = jnp.zeros((share, feat), BF16)
    wide[:, pl.ds(feat, 8)] = jnp.transpose(stacked).astype(BF16)
    load_d.wait()
    for b in range(blocks):
        dec_t[b] = jnp.transpose(dec[pl.ds(b * stride, stride), :])
    load_w.wait()

    def take_rows(step, carry):
        source = lax.rem(me + step, peers)
        copy_a(source, source).wait_recv()
        return carry

    lax.fori_loop(1, peers, take_rows, 0)

    arrived = inbox[...].astype(F32)
    x = arrived[:, 0:tok, :].reshape(rows, feat)
    index_t = jnp.transpose(arrived[:, tok : 2 * tok, :].reshape(rows, feat))
    squares = jnp.sum(jnp.sum(x * x, axis=0, keepdims=True), axis=1, keepdims=True)
    scale = lax.rsqrt(squares / (rows * feat) + EPSILON)
    normed = x * scale
    vec = decb_ref[...]
    encoder_in = (normed - vec).astype(BF16)
    ones = (lax.broadcasted_iota(jnp.int32, (rows, feat), 1) < 3).astype(F32).astype(BF16)
    joint = jnp.concatenate([encoder_in, ones], axis=1)

    wanted = (lax.broadcasted_iota(jnp.int32, (blocks, rows), 0) + my_d * blocks).astype(F32)
    found = jnp.zeros((blocks, rows), F32)
    for k in range(top):
        found = jnp.where(index_t[top + k : top + k + 1, :] == wanted, index_t[k : k + 1, :], found)
    offs[...] = found.astype(jnp.int32)

    latent = lax.broadcasted_iota(jnp.int32, (stride, rows), 0)
    acc[...] = jnp.zeros_like(acc)

    def encode(b, carry):
        here = pl.ds(pl.multiple_of(b * stride, stride), stride)
        scores = lax.dot_general(
            wide[here, :], joint, (((1,), (1,)), ((), ())), preferred_element_type=F32
        )
        block = jnp.where(latent == offs[pl.ds(b, 1), :], scores, 0.0).astype(BF16)
        codes[here, :] = block
        acc[...] += jnp.dot(dec_t[b], block, preferred_element_type=F32)
        return carry

    lax.fori_loop(0, blocks, encode, 0, unroll=2)

    partner = pltpu.make_async_remote_copy(
        src_ref=acc, dst_ref=acc_in, send_sem=send_b, recv_sem=recv_b,
        device_id={"head": my_h, "dp": 1 - my_d}, device_id_type=MESH,
    )
    partner.start()
    center = jnp.sum(x, axis=0, keepdims=True) * scale / rows
    spread = jnp.sum(jnp.square(normed - center))
    partner.wait_recv()

    recon_normed = jnp.transpose(acc[...] + acc_in[...]) + vec
    rebuilt[...] = recon_normed / scale
    for h in range(heads):
        start = pl.multiple_of((h * shards + my_d) * tok, 8)
        part = rebuilt[pl.ds(start, tok), :]
        extra = reply.shape[1] - tok
        if extra:
            part = jnp.concatenate([part, jnp.zeros((extra, feat), F32)], axis=0)
        reply[h] = part.astype(BF16)

    def copy_c(peer, slot):
        return pltpu.make_async_remote_copy(
            src_ref=reply.at[peer],
            dst_ref=back.at[slot],
            send_sem=send_c.at[peer],
            recv_sem=recv_c.at[slot],
            device_id={"head": peer, "dp": my_d},
            device_id_type=MESH,
        )

    def send_back(step, carry):
        copy_c(lax.rem(my_h + step, heads), my_h).start()
        return carry

    lax.fori_loop(1, heads, send_back, 0)
    back[my_h] = reply[my_h]

    mismatch = recon_normed - normed
    error = (mismatch * (latents / (rows * top))).astype(BF16)
    expl_ref[0] = 1.0 - jnp.sum(mismatch * mismatch) / spread

    def gradient(b, carry):
        here = pl.ds(pl.multiple_of(b * stride, stride), stride)
        grad_ref[0, here, :] = jnp.dot(codes[here, :], error, preferred_element_type=F32)
        return carry

    lax.fori_loop(0, blocks, gradient, 0, unroll=2)

    def take_back(step, carry):
        source = lax.rem(my_h + step, heads)
        copy_c(source, source).wait_recv()
        return carry

    lax.fori_loop(1, heads, take_back, 0)
    for h in range(heads):
        result[pl.ds(h, tok, stride=heads), :] = back[h].astype(F32)[0:tok, :]
    recon_ref[...] = result[...].reshape(tok, heads, feat).astype(BF16)

    partner.wait_send()

    def sent_a(step, carry):
        copy_a(lax.rem(me + step, peers), me).wait_send()
        return carry

    lax.fori_loop(1, peers, sent_a, 0)

    def sent_c(step, carry):
        copy_c(lax.rem(my_h + step, heads), my_h).wait_send()
        return carry

    lax.fori_loop(1, heads, sent_c, 0)


def per_device(heads, shards, head_outputs, active, enc_weight, enc_bias, dec_weight, dec_bias):
    tok, _, feat = head_outputs.shape
    latents = enc_weight.shape[1]
    top = active.shape[2]
    share = latents // shards
    stride = latents // top
    blocks = share // stride
    peers = heads * shards
    rows = peers * tok
    back_rows = round_up(tok, PAD)
    vmem = pl.BlockSpec(memory_space=pltpu.VMEM)
    anywhere = pl.BlockSpec(memory_space=pl.ANY)
    return pl.pallas_call(
        functools.partial(step_kernel, heads, shards),
        out_shape=(
            jax.ShapeDtypeStruct((tok, heads, feat), BF16),
            jax.ShapeDtypeStruct((1,), F32),
            jax.ShapeDtypeStruct((1, share, feat), F32),
        ),
        in_specs=[vmem, vmem, anywhere, anywhere, anywhere, vmem],
        out_specs=(vmem, pl.BlockSpec(memory_space=pltpu.SMEM), vmem),
        scratch_shapes=[
            pltpu.VMEM((tok * heads, feat), F32),
            pltpu.VMEM((tok * heads, feat), F32),
            pltpu.VMEM((heads, 2 * tok, feat), BF16),
            pltpu.VMEM((peers, 2 * tok, feat), BF16),
            pltpu.VMEM((share, 2 * feat), BF16),
            pltpu.VMEM((share, feat), BF16),
            pltpu.VMEM((blocks, feat, stride), BF16),
            pltpu.VMEM((1, share), F32),
            pltpu.VMEM((share, rows), BF16),
            pltpu.VMEM((blocks, rows), jnp.int32),
            pltpu.VMEM((feat, rows), F32),
            pltpu.VMEM((feat, rows), F32),
            pltpu.VMEM((rows, feat), F32),
            pltpu.VMEM((heads, back_rows, feat), BF16),
            pltpu.VMEM((heads, back_rows, feat), BF16),
            pltpu.VMEM((tok * heads, feat), F32),
            pltpu.SemaphoreType.DMA((3,)),
            pltpu.SemaphoreType.DMA((peers,)),
            pltpu.SemaphoreType.DMA((peers,)),
            pltpu.SemaphoreType.DMA,
            pltpu.SemaphoreType.DMA,
            pltpu.SemaphoreType.DMA((heads,)),
            pltpu.SemaphoreType.DMA((heads,)),
        ],
        compiler_params=pltpu.CompilerParams(
            collective_id=0, has_side_effects=True, vmem_limit_bytes=48 * 1024 * 1024
        ),
    )(head_outputs, active, enc_weight, enc_bias, dec_weight, dec_bias)


def solution(mesh):
    placed = (
        P(("groups", "head", "dp"), None, None),
        P(("groups", "head", "dp"), None, None),
        P(("groups", "head"), None, None),
        P(("groups", "head"), None),
        P(("groups", "head"), None, None),
        P(("groups", "head"), None),
    )
    return jax.shard_map(
        functools.partial(per_device, mesh.shape["head"], mesh.shape["dp"]),
        mesh=mesh,
        in_specs=placed,
        out_specs=(
            P(("groups", "head", "dp"), None, None),
            P(("groups", "head")),
            P(("groups", "head"), "dp", None),
        ),
        check_vma=False,
    )
```

```python
import functools

import jax
import jax.numpy as jnp
from jax import lax
from jax.experimental import pallas as pl
from jax.experimental.pallas import tpu as pltpu
from jax.sharding import PartitionSpec as P

EPSILON = 1e-06
F32 = jnp.float32
BF16 = jnp.bfloat16
MESH = pl.DeviceIdType.MESH
PAD = 16
PARTS = 4


def round_up(value, unit):
    return (value + unit - 1) // unit * unit


def step_kernel(
    heads, shards, x_hbm, act_hbm, encw_ref, encb_ref, decw_ref, decb_hbm,
    recon_ref, expl_ref, grad_ref,
    x_ref, act_ref, decb_ref, xs, acts, msg, inbox, wide, dec, dec_t, bias, codes, offs, acc, acc_in, rebuilt, reply, back, result,
    local_sem, send_a, recv_a, send_b, recv_b, send_c, recv_c,
):
    tok = x_ref.shape[0]
    feat = x_ref.shape[2]
    top = act_ref.shape[2]
    latents = encw_ref.shape[1]
    share = latents // shards
    stride = latents // top
    shift = stride.bit_length() - 1
    blocks = share // stride
    peers = heads * shards
    rows = peers * tok
    my_h = lax.axis_index("head")
    my_d = lax.axis_index("dp")
    me = my_h * shards + my_d

    first = pl.multiple_of(my_d * share, share)
    load_w = pltpu.make_async_copy(
        encw_ref.at[0, pl.ds(first, share), :], wide.at[:, pl.ds(0, feat)], local_sem.at[0]
    )
    load_d = pltpu.make_async_copy(decw_ref.at[0, pl.ds(first, share), :], dec, local_sem.at[1])
    load_b = pltpu.make_async_copy(encb_ref.at[:, pl.ds(first, share)], bias, local_sem.at[2])
    load_x = pltpu.make_async_copy(x_hbm, x_ref, local_sem.at[3])
    load_a = pltpu.make_async_copy(act_hbm, act_ref, local_sem.at[4])
    load_v = pltpu.make_async_copy(decb_hbm, decb_ref, local_sem.at[5])
    load_x.start()
    load_a.start()
    load_b.start()
    load_v.start()
    load_d.start()
    load_w.start()

    barrier = pltpu.get_barrier_semaphore()

    def greet(step, carry):
        peer = lax.rem(me + step, peers)
        pl.semaphore_signal(
            barrier, inc=1,
            device_id={"head": peer // shards, "dp": lax.rem(peer, shards)}, device_id_type=MESH,
        )
        return carry

    lax.fori_loop(1, peers, greet, 0)

    load_x.wait()
    load_a.wait()
    xs[...] = x_ref[...].astype(F32).reshape(tok * heads, feat)
    picked = act_ref[...].reshape(tok * heads, top)
    acts[...] = jnp.zeros_like(acts)
    acts[:, 0:top] = (picked & (stride - 1)).astype(F32)
    acts[:, top : 2 * top] = (picked >> shift).astype(F32)
    for h in range(heads):
        both = jnp.concatenate(
            [xs[pl.ds(h, tok, stride=heads), :], acts[pl.ds(h, tok, stride=heads), :]], axis=0
        )
        msg[h] = both.astype(BF16)
    pl.semaphore_wait(barrier, peers - 1)

    def copy_a(peer, slot):
        return pltpu.make_async_remote_copy(
            src_ref=msg.at[peer // shards],
            dst_ref=inbox.at[slot],
            send_sem=send_a.at[peer],
            recv_sem=recv_a.at[slot],
            device_id={"head": peer // shards, "dp": lax.rem(peer, shards)},
            device_id_type=MESH,
        )

    def send_rows(step, carry):
        copy_a(lax.rem(me + step, peers), me).start()
        return carry

    lax.fori_loop(1, peers, send_rows, 0)
    inbox[me] = msg[my_h]

    load_b.wait()
    load_v.wait()
    whole = bias[...]
    high = whole.astype(BF16).astype(F32)
    mid = (whole - high).astype(BF16).astype(F32)
    low = whole - high - mid
    stacked = jnp.concatenate([high, mid, low, jnp.zeros((5, share), F32)], axis=0)
    wide[:, pl.ds(feat, feat)] = jnp.zeros((share, feat), BF16)
    wide[:, pl.ds(feat, 8)] = jnp.transpose(stacked).astype(BF16)
    load_d.wait()
    for b in range(blocks):
        dec_t[b] = jnp.transpose(dec[pl.ds(b * stride, stride), :])
    load_w.wait()

    def take_rows(step, carry):
        source = lax.rem(me - step + peers, peers)
        copy_a(source, source).wait_recv()
        return carry

    lax.fori_loop(1, peers, take_rows, 0)

    arrived = inbox[...].astype(F32)
    x = arrived[:, 0:tok, :].reshape(rows, feat)
    index_t = jnp.transpose(arrived[:, tok : 2 * tok, :].reshape(rows, feat))
    squares = jnp.sum(jnp.sum(x * x, axis=0, keepdims=True), axis=1, keepdims=True)
    scale = lax.rsqrt(squares / (rows * feat) + EPSILON)
    normed = x * scale
    vec = decb_ref[...]
    encoder_in = (normed - vec).astype(BF16)
    ones = (lax.broadcasted_iota(jnp.int32, (rows, feat), 1) < 3).astype(F32).astype(BF16)
    joint = jnp.concatenate([encoder_in, ones], axis=1)

    wanted = (lax.broadcasted_iota(jnp.int32, (blocks, rows), 0) + my_d * blocks).astype(F32)
    found = jnp.zeros((blocks, rows), F32)
    for k in range(top):
        found = jnp.where(index_t[top + k : top + k + 1, :] == wanted, index_t[k : k + 1, :], found)
    offs[...] = found.astype(jnp.int32)

    latent = lax.broadcasted_iota(jnp.int32, (stride, rows), 0)

    def encode(b, carry):
        here = pl.ds(pl.multiple_of(b * stride, stride), stride)
        scores = lax.dot_general(
            wide[here, :], joint, (((1,), (1,)), ((), ())), preferred_element_type=F32
        )
        block = jnp.where(latent == offs[pl.ds(b, 1), :], scores, 0.0).astype(BF16)
        codes[here, :] = block
        return carry

    lax.fori_loop(0, blocks, encode, 0, unroll=4)
    total = jnp.dot(dec_t[0], codes[0:stride, :], preferred_element_type=F32)
    for b in range(1, blocks):
        here = pl.ds(b * stride, stride)
        total += jnp.dot(dec_t[b], codes[here, :], preferred_element_type=F32)
    acc[...] = total

    partner = pltpu.make_async_remote_copy(
        src_ref=acc, dst_ref=acc_in, send_sem=send_b, recv_sem=recv_b,
        device_id={"head": my_h, "dp": 1 - my_d}, device_id_type=MESH,
    )
    partner.start()
    center = jnp.sum(x, axis=0, keepdims=True) * scale / rows
    spread = jnp.sum(jnp.square(normed - center))
    partner.wait_recv()

    recon_normed = jnp.transpose(acc[...] + acc_in[...]) + vec
    rebuilt[...] = recon_normed / scale
    for h in range(heads):
        start = pl.multiple_of((h * shards + my_d) * tok, 8)
        part = rebuilt[pl.ds(start, tok), :]
        extra = reply.shape[1] - tok
        if extra:
            part = jnp.concatenate([part, jnp.zeros((extra, feat), F32)], axis=0)
        reply[h] = part.astype(BF16)

    def copy_c(peer, slot):
        return pltpu.make_async_remote_copy(
            src_ref=reply.at[peer],
            dst_ref=back.at[slot],
            send_sem=send_c.at[peer],
            recv_sem=recv_c.at[slot],
            device_id={"head": peer, "dp": my_d},
            device_id_type=MESH,
        )

    def send_back(step, carry):
        copy_c(lax.rem(my_h + step, heads), my_h).start()
        return carry

    lax.fori_loop(1, heads, send_back, 0)
    back[my_h] = reply[my_h]

    mismatch = recon_normed - normed
    error = (mismatch * (latents / (rows * top))).astype(BF16)
    expl_ref[0] = 1.0 - jnp.sum(mismatch * mismatch) / spread

    def gradient(b, carry):
        here = pl.ds(pl.multiple_of(b * stride, stride), stride)
        grad_ref[0, here, :] = jnp.dot(codes[here, :], error, preferred_element_type=F32)
        return carry

    lax.fori_loop(0, blocks, gradient, 0, unroll=4)

    def take_back(step, carry):
        source = lax.rem(my_h - step + heads, heads)
        copy_c(source, source).wait_recv()
        return carry

    lax.fori_loop(1, heads, take_back, 0)
    for h in range(heads):
        result[pl.ds(h, tok, stride=heads), :] = back[h].astype(F32)[0:tok, :]
    recon_ref[...] = result[...].reshape(tok, heads, feat).astype(BF16)

    partner.wait_send()

    def sent_a(step, carry):
        copy_a(lax.rem(me + step, peers), me).wait_send()
        return carry

    lax.fori_loop(1, peers, sent_a, 0)

    def sent_c(step, carry):
        copy_c(lax.rem(my_h + step, heads), my_h).wait_send()
        return carry

    lax.fori_loop(1, heads, sent_c, 0)


def store_kernel(recon_in, expl_in, grad_in, recon_ref, expl_ref, grad_ref, sems):
    size = grad_in.shape[1] // PARTS
    copies = [pltpu.make_async_copy(recon_in, recon_ref, sems.at[PARTS])]
    for part in range(PARTS):
        here = pl.ds(part * size, size)
        copies.append(
            pltpu.make_async_copy(grad_in.at[:, here, :], grad_ref.at[:, here, :], sems.at[part])
        )
    for copy in copies:
        copy.start()
    expl_ref[0] = expl_in[0]
    for copy in copies:
        copy.wait()


def per_device(heads, shards, head_outputs, active, enc_weight, enc_bias, dec_weight, dec_bias):
    tok, _, feat = head_outputs.shape
    latents = enc_weight.shape[1]
    top = active.shape[2]
    share = latents // shards
    stride = latents // top
    blocks = share // stride
    peers = heads * shards
    rows = peers * tok
    back_rows = round_up(tok, PAD)
    vmem = pl.BlockSpec(memory_space=pltpu.VMEM)
    hbm = pl.BlockSpec(memory_space=pltpu.HBM)
    results = pl.pallas_call(
        functools.partial(step_kernel, heads, shards),
        out_shape=(
            jax.ShapeDtypeStruct((tok, heads, feat), BF16),
            jax.ShapeDtypeStruct((1,), F32),
            jax.ShapeDtypeStruct((1, share, feat), F32),
        ),
        in_specs=[hbm] * 6,
        out_specs=(vmem, pl.BlockSpec(memory_space=pltpu.SMEM), vmem),
        scratch_shapes=[
            pltpu.VMEM((tok, heads, feat), BF16),
            pltpu.VMEM((tok, heads, top), jnp.int32),
            pltpu.VMEM((1, feat), F32),
            pltpu.VMEM((tok * heads, feat), F32),
            pltpu.VMEM((tok * heads, feat), F32),
            pltpu.VMEM((heads, 2 * tok, feat), BF16),
            pltpu.VMEM((peers, 2 * tok, feat), BF16),
            pltpu.VMEM((share, 2 * feat), BF16),
            pltpu.VMEM((share, feat), BF16),
            pltpu.VMEM((blocks, feat, stride), BF16),
            pltpu.VMEM((1, share), F32),
            pltpu.VMEM((share, rows), BF16),
            pltpu.VMEM((blocks, rows), jnp.int32),
            pltpu.VMEM((feat, rows), F32),
            pltpu.VMEM((feat, rows), F32),
            pltpu.VMEM((rows, feat), F32),
            pltpu.VMEM((heads, back_rows, feat), BF16),
            pltpu.VMEM((heads, back_rows, feat), BF16),
            pltpu.VMEM((tok * heads, feat), F32),
            pltpu.SemaphoreType.DMA((6,)),
            pltpu.SemaphoreType.DMA((peers,)),
            pltpu.SemaphoreType.DMA((peers,)),
            pltpu.SemaphoreType.DMA,
            pltpu.SemaphoreType.DMA,
            pltpu.SemaphoreType.DMA((heads,)),
            pltpu.SemaphoreType.DMA((heads,)),
        ],
        compiler_params=pltpu.CompilerParams(
            collective_id=0, has_side_effects=True, vmem_limit_bytes=48 * 1024 * 1024
        ),
    )(*(
        pltpu.with_memory_space_constraint(operand, pltpu.HBM)
        for operand in (head_outputs, active, enc_weight, enc_bias, dec_weight, dec_bias)
    ))
    smem = pl.BlockSpec(memory_space=pltpu.SMEM)
    return pl.pallas_call(
        store_kernel,
        out_shape=tuple(jax.ShapeDtypeStruct(r.shape, r.dtype) for r in results),
        in_specs=[vmem, smem, vmem],
        out_specs=(hbm, smem, hbm),
        scratch_shapes=[pltpu.SemaphoreType.DMA((1 + PARTS,))],
        compiler_params=pltpu.CompilerParams(vmem_limit_bytes=16 * 1024 * 1024),
    )(*results)


def solution(mesh):
    placed = (
        P(("groups", "head", "dp"), None, None),
        P(("groups", "head", "dp"), None, None),
        P(("groups", "head"), None, None),
        P(("groups", "head"), None),
        P(("groups", "head"), None, None),
        P(("groups", "head"), None),
    )
    return jax.shard_map(
        functools.partial(per_device, mesh.shape["head"], mesh.shape["dp"]),
        mesh=mesh,
        in_specs=placed,
        out_specs=(
            P(("groups", "head", "dp"), None, None),
            P(("groups", "head")),
            P(("groups", "head"), "dp", None),
        ),
        check_vma=False,
    )
```

```python
import functools

import jax
import jax.numpy as jnp
from jax import lax
from jax.experimental import pallas as pl
from jax.experimental.pallas import tpu as pltpu
from jax.sharding import PartitionSpec as P

EPSILON = 1e-06
F32 = jnp.float32
BF16 = jnp.bfloat16
MESH = pl.DeviceIdType.MESH
PAD = 16
PARTS = 4


def round_up(value, unit):
    return (value + unit - 1) // unit * unit


def step_kernel(
    heads, shards, x_hbm, act_hbm, encw_ref, encb_ref, decw_ref, decb_hbm,
    recon_ref, expl_ref, grad_ref,
    x_ref, act_ref, decb_ref, xs, acts, msg, inbox, wide, dec, dec_t, bias, codes, offs, acc, acc_in, rebuilt, reply, back, result,
    local_sem, send_a, recv_a, send_f, send_b, recv_b, send_c, recv_c,
):
    tok = x_ref.shape[0]
    feat = x_ref.shape[2]
    top = act_ref.shape[2]
    latents = encw_ref.shape[1]
    share = latents // shards
    stride = latents // top
    shift = stride.bit_length() - 1
    blocks = share // stride
    peers = heads * shards
    rows = peers * tok
    my_h = lax.axis_index("head")
    my_d = lax.axis_index("dp")
    me = my_h * shards + my_d

    first = pl.multiple_of(my_d * share, share)
    load_w = pltpu.make_async_copy(
        encw_ref.at[0, pl.ds(first, share), :], wide.at[:, pl.ds(0, feat)], local_sem.at[0]
    )
    load_d = pltpu.make_async_copy(decw_ref.at[0, pl.ds(first, share), :], dec, local_sem.at[1])
    load_b = pltpu.make_async_copy(encb_ref.at[:, pl.ds(first, share)], bias, local_sem.at[2])
    load_x = pltpu.make_async_copy(x_hbm, x_ref, local_sem.at[3])
    load_a = pltpu.make_async_copy(act_hbm, act_ref, local_sem.at[4])
    load_v = pltpu.make_async_copy(decb_hbm, decb_ref, local_sem.at[5])
    load_x.start()
    load_a.start()
    load_b.start()
    load_v.start()
    load_d.start()
    load_w.start()

    barrier = pltpu.get_barrier_semaphore()

    def greet(step, carry):
        pl.semaphore_signal(
            barrier, inc=1,
            device_id={"head": lax.rem(my_h + step, heads), "dp": my_d}, device_id_type=MESH,
        )
        return carry

    lax.fori_loop(1, heads, greet, 0)
    pl.semaphore_signal(
        barrier, inc=1, device_id={"head": my_h, "dp": 1 - my_d}, device_id_type=MESH
    )

    load_x.wait()
    load_a.wait()
    xs[...] = x_ref[...].astype(F32).reshape(tok * heads, feat)
    picked = act_ref[...].reshape(tok * heads, top)
    acts[...] = jnp.zeros_like(acts)
    acts[:, 0:top] = (picked & (stride - 1)).astype(F32)
    acts[:, top : 2 * top] = (picked >> shift).astype(F32)
    for h in range(heads):
        both = jnp.concatenate(
            [xs[pl.ds(h, tok, stride=heads), :], acts[pl.ds(h, tok, stride=heads), :]], axis=0
        )
        msg[h] = both.astype(BF16)
    pl.semaphore_wait(barrier, heads)

    def copy_a(peer, sender):
        return pltpu.make_async_remote_copy(
            src_ref=msg.at[peer],
            dst_ref=inbox.at[sender * shards + my_d],
            send_sem=send_a.at[peer],
            recv_sem=recv_a.at[sender * shards + my_d],
            device_id={"head": peer, "dp": my_d},
            device_id_type=MESH,
        )

    def forward(sender, side):
        slot = sender * shards + side
        return pltpu.make_async_remote_copy(
            src_ref=inbox.at[slot],
            dst_ref=inbox.at[slot],
            send_sem=send_f.at[sender],
            recv_sem=recv_a.at[slot],
            device_id={"head": my_h, "dp": 1 - my_d},
            device_id_type=MESH,
        )

    def send_rows(step, carry):
        copy_a(lax.rem(my_h + step, heads), my_h).start()
        return carry

    lax.fori_loop(1, heads, send_rows, 0)
    inbox[me] = msg[my_h]
    forward(my_h, my_d).start()

    load_b.wait()
    load_v.wait()
    whole = bias[...]
    high = whole.astype(BF16).astype(F32)
    mid = (whole - high).astype(BF16).astype(F32)
    low = whole - high - mid
    stacked = jnp.concatenate([high, mid, low, jnp.zeros((5, share), F32)], axis=0)
    wide[:, pl.ds(feat, feat)] = jnp.zeros((share, feat), BF16)
    wide[:, pl.ds(feat, 8)] = jnp.transpose(stacked).astype(BF16)
    load_d.wait()
    for b in range(blocks):
        dec_t[b] = jnp.transpose(dec[pl.ds(b * stride, stride), :])
    load_w.wait()

    def take_rows(step, carry):
        source = lax.rem(my_h - step + heads, heads)
        copy_a(source, source).wait_recv()
        forward(source, my_d).start()
        return carry

    lax.fori_loop(1, heads, take_rows, 0)

    def take_forwarded(step, carry):
        forward(lax.rem(my_h - step + heads, heads), 1 - my_d).wait_recv()
        return carry

    lax.fori_loop(0, heads, take_forwarded, 0)

    arrived = inbox[...].astype(F32)
    x = arrived[:, 0:tok, :].reshape(rows, feat)
    index_t = jnp.transpose(arrived[:, tok : 2 * tok, :].reshape(rows, feat))
    squares = jnp.sum(jnp.sum(x * x, axis=0, keepdims=True), axis=1, keepdims=True)
    scale = lax.rsqrt(squares / (rows * feat) + EPSILON)
    normed = x * scale
    vec = decb_ref[...]
    encoder_in = (normed - vec).astype(BF16)
    ones = (lax.broadcasted_iota(jnp.int32, (rows, feat), 1) < 3).astype(F32).astype(BF16)
    joint = jnp.concatenate([encoder_in, ones], axis=1)

    wanted = (lax.broadcasted_iota(jnp.int32, (blocks, rows), 0) + my_d * blocks).astype(F32)
    found = jnp.zeros((blocks, rows), F32)
    for k in range(top):
        found = jnp.where(index_t[top + k : top + k + 1, :] == wanted, index_t[k : k + 1, :], found)
    offs[...] = found.astype(jnp.int32)

    latent = lax.broadcasted_iota(jnp.int32, (stride, rows), 0)

    def encode(b, carry):
        here = pl.ds(pl.multiple_of(b * stride, stride), stride)
        scores = lax.dot_general(
            wide[here, :], joint, (((1,), (1,)), ((), ())), preferred_element_type=F32
        )
        block = jnp.where(latent == offs[pl.ds(b, 1), :], scores, 0.0).astype(BF16)
        codes[here, :] = block
        return carry

    lax.fori_loop(0, blocks, encode, 0, unroll=4)
    total = jnp.dot(dec_t[0], codes[0:stride, :], preferred_element_type=F32)
    for b in range(1, blocks):
        here = pl.ds(b * stride, stride)
        total += jnp.dot(dec_t[b], codes[here, :], preferred_element_type=F32)
    acc[...] = total

    partner = pltpu.make_async_remote_copy(
        src_ref=acc, dst_ref=acc_in, send_sem=send_b, recv_sem=recv_b,
        device_id={"head": my_h, "dp": 1 - my_d}, device_id_type=MESH,
    )
    partner.start()
    center = jnp.sum(x, axis=0, keepdims=True) * scale / rows
    spread = jnp.sum(jnp.square(normed - center))
    partner.wait_recv()

    recon_normed = jnp.transpose(acc[...] + acc_in[...]) + vec
    rebuilt[...] = recon_normed / scale
    for h in range(heads):
        start = pl.multiple_of((h * shards + my_d) * tok, 8)
        part = rebuilt[pl.ds(start, tok), :]
        extra = reply.shape[1] - tok
        if extra:
            part = jnp.concatenate([part, jnp.zeros((extra, feat), F32)], axis=0)
        reply[h] = part.astype(BF16)

    def copy_c(peer, slot):
        return pltpu.make_async_remote_copy(
            src_ref=reply.at[peer],
            dst_ref=back.at[slot],
            send_sem=send_c.at[peer],
            recv_sem=recv_c.at[slot],
            device_id={"head": peer, "dp": my_d},
            device_id_type=MESH,
        )

    def send_back(step, carry):
        copy_c(lax.rem(my_h + step, heads), my_h).start()
        return carry

    lax.fori_loop(1, heads, send_back, 0)
    back[my_h] = reply[my_h]

    mismatch = recon_normed - normed
    error = (mismatch * (latents / (rows * top))).astype(BF16)
    expl_ref[0] = 1.0 - jnp.sum(mismatch * mismatch) / spread

    def gradient(b, carry):
        here = pl.ds(pl.multiple_of(b * stride, stride), stride)
        grad_ref[0, here, :] = jnp.dot(codes[here, :], error, preferred_element_type=F32)
        return carry

    lax.fori_loop(0, blocks, gradient, 0, unroll=4)

    def take_back(step, carry):
        source = lax.rem(my_h - step + heads, heads)
        copy_c(source, source).wait_recv()
        return carry

    lax.fori_loop(1, heads, take_back, 0)
    for h in range(heads):
        result[pl.ds(h, tok, stride=heads), :] = back[h].astype(F32)[0:tok, :]
    recon_ref[...] = result[...].reshape(tok, heads, feat).astype(BF16)

    partner.wait_send()

    def sent_a(step, carry):
        peer = lax.rem(my_h + step, heads)
        copy_a(peer, my_h).wait_send()
        forward(peer, my_d).wait_send()
        return carry

    lax.fori_loop(1, heads, sent_a, 0)
    forward(my_h, my_d).wait_send()

    def sent_c(step, carry):
        copy_c(lax.rem(my_h + step, heads), my_h).wait_send()
        return carry

    lax.fori_loop(1, heads, sent_c, 0)


def store_kernel(recon_in, expl_in, grad_in, recon_ref, expl_ref, grad_ref, sems):
    size = grad_in.shape[1] // PARTS
    copies = [pltpu.make_async_copy(recon_in, recon_ref, sems.at[PARTS])]
    for part in range(PARTS):
        here = pl.ds(part * size, size)
        copies.append(
            pltpu.make_async_copy(grad_in.at[:, here, :], grad_ref.at[:, here, :], sems.at[part])
        )
    for copy in copies:
        copy.start()
    expl_ref[0] = expl_in[0]
    for copy in copies:
        copy.wait()


def per_device(heads, shards, head_outputs, active, enc_weight, enc_bias, dec_weight, dec_bias):
    tok, _, feat = head_outputs.shape
    latents = enc_weight.shape[1]
    top = active.shape[2]
    share = latents // shards
    stride = latents // top
    blocks = share // stride
    peers = heads * shards
    rows = peers * tok
    back_rows = round_up(tok, PAD)
    vmem = pl.BlockSpec(memory_space=pltpu.VMEM)
    hbm = pl.BlockSpec(memory_space=pltpu.HBM)
    results = pl.pallas_call(
        functools.partial(step_kernel, heads, shards),
        out_shape=(
            jax.ShapeDtypeStruct((tok, heads, feat), BF16),
            jax.ShapeDtypeStruct((1,), F32),
            jax.ShapeDtypeStruct((1, share, feat), F32),
        ),
        in_specs=[hbm] * 6,
        out_specs=(vmem, pl.BlockSpec(memory_space=pltpu.SMEM), vmem),
        scratch_shapes=[
            pltpu.VMEM((tok, heads, feat), BF16),
            pltpu.VMEM((tok, heads, top), jnp.int32),
            pltpu.VMEM((1, feat), F32),
            pltpu.VMEM((tok * heads, feat), F32),
            pltpu.VMEM((tok * heads, feat), F32),
            pltpu.VMEM((heads, 2 * tok, feat), BF16),
            pltpu.VMEM((peers, 2 * tok, feat), BF16),
            pltpu.VMEM((share, 2 * feat), BF16),
            pltpu.VMEM((share, feat), BF16),
            pltpu.VMEM((blocks, feat, stride), BF16),
            pltpu.VMEM((1, share), F32),
            pltpu.VMEM((share, rows), BF16),
            pltpu.VMEM((blocks, rows), jnp.int32),
            pltpu.VMEM((feat, rows), F32),
            pltpu.VMEM((feat, rows), F32),
            pltpu.VMEM((rows, feat), F32),
            pltpu.VMEM((heads, back_rows, feat), BF16),
            pltpu.VMEM((heads, back_rows, feat), BF16),
            pltpu.VMEM((tok * heads, feat), F32),
            pltpu.SemaphoreType.DMA((6,)),
            pltpu.SemaphoreType.DMA((heads,)),
            pltpu.SemaphoreType.DMA((peers,)),
            pltpu.SemaphoreType.DMA((heads,)),
            pltpu.SemaphoreType.DMA,
            pltpu.SemaphoreType.DMA,
            pltpu.SemaphoreType.DMA((heads,)),
            pltpu.SemaphoreType.DMA((heads,)),
        ],
        compiler_params=pltpu.CompilerParams(
            collective_id=0, has_side_effects=True, vmem_limit_bytes=48 * 1024 * 1024
        ),
    )(*(
        pltpu.with_memory_space_constraint(operand, pltpu.HBM)
        for operand in (head_outputs, active, enc_weight, enc_bias, dec_weight, dec_bias)
    ))
    smem = pl.BlockSpec(memory_space=pltpu.SMEM)
    return pl.pallas_call(
        store_kernel,
        out_shape=tuple(jax.ShapeDtypeStruct(r.shape, r.dtype) for r in results),
        in_specs=[vmem, smem, vmem],
        out_specs=(hbm, smem, hbm),
        scratch_shapes=[pltpu.SemaphoreType.DMA((1 + PARTS,))],
        compiler_params=pltpu.CompilerParams(vmem_limit_bytes=16 * 1024 * 1024),
    )(*results)


def solution(mesh):
    placed = (
        P(("groups", "head", "dp"), None, None),
        P(("groups", "head", "dp"), None, None),
        P(("groups", "head"), None, None),
        P(("groups", "head"), None),
        P(("groups", "head"), None, None),
        P(("groups", "head"), None),
    )
    return jax.shard_map(
        functools.partial(per_device, mesh.shape["head"], mesh.shape["dp"]),
        mesh=mesh,
        in_specs=placed,
        out_specs=(
            P(("groups", "head", "dp"), None, None),
            P(("groups", "head")),
            P(("groups", "head"), "dp", None),
        ),
        check_vma=False,
    )
```

```python
import functools

import jax
import jax.numpy as jnp
from jax import lax
from jax.experimental import pallas as pl
from jax.experimental.pallas import tpu as pltpu
from jax.sharding import PartitionSpec as P

EPSILON = 1e-06
F32 = jnp.float32
BF16 = jnp.bfloat16
MESH = pl.DeviceIdType.MESH
PAD = 16
PARTS = 4


def round_up(value, unit):
    return (value + unit - 1) // unit * unit


def step_kernel(
    heads, shards, x_hbm, act_hbm, encw_ref, encb_ref, decw_ref, decb_hbm,
    recon_ref, expl_ref, grad_ref,
    x_ref, act_ref, decb_ref, xs, acts, msg, inbox, wide, dec, dec_t, bias, codes, offs, acc, acc_in, rebuilt, reply, back, result,
    local_sem, send_a, recv_a, send_f, send_b, recv_b, send_c, recv_c,
):
    tok = x_ref.shape[0]
    feat = x_ref.shape[2]
    top = act_ref.shape[2]
    latents = encw_ref.shape[1]
    share = latents // shards
    stride = latents // top
    shift = stride.bit_length() - 1
    blocks = share // stride
    peers = heads * shards
    rows = peers * tok
    my_h = lax.axis_index("head")
    my_d = lax.axis_index("dp")
    me = my_h * shards + my_d

    first = pl.multiple_of(my_d * share, share)
    load_w = pltpu.make_async_copy(
        encw_ref.at[0, pl.ds(first, share), :], wide.at[:, pl.ds(0, feat)], local_sem.at[0]
    )
    load_d = pltpu.make_async_copy(decw_ref.at[0, pl.ds(first, share), :], dec, local_sem.at[1])
    load_b = pltpu.make_async_copy(encb_ref.at[:, pl.ds(first, share)], bias, local_sem.at[2])
    load_x = pltpu.make_async_copy(x_hbm, x_ref, local_sem.at[3])
    load_a = pltpu.make_async_copy(act_hbm, act_ref, local_sem.at[4])
    load_v = pltpu.make_async_copy(decb_hbm, decb_ref, local_sem.at[5])
    load_x.start()
    load_a.start()
    load_b.start()
    load_v.start()
    load_d.start()
    load_w.start()

    barrier = pltpu.get_barrier_semaphore()

    def greet(step, carry):
        pl.semaphore_signal(
            barrier, inc=1,
            device_id={"head": lax.rem(my_h + step, heads), "dp": my_d}, device_id_type=MESH,
        )
        return carry

    lax.fori_loop(1, heads, greet, 0)
    pl.semaphore_signal(
        barrier, inc=1, device_id={"head": my_h, "dp": 1 - my_d}, device_id_type=MESH
    )

    load_x.wait()
    load_a.wait()
    xs[...] = x_ref[...].astype(F32).reshape(tok * heads, feat)
    picked = act_ref[...].reshape(tok * heads, top)
    acts[...] = jnp.zeros_like(acts)
    half = stride // 2
    band = picked >> shift
    inner = ((picked & (half - 1)) + half) << (band & 15)
    code = inner.astype(F32) * jnp.where(band >= 16, 65536.0, 1.0)
    acts[:, 0:top] = jnp.where((picked & half) != 0, -code, code)
    for h in range(heads):
        index_rows = acts[pl.ds(h, tok, stride=heads), :]
        packed = index_rows[0:8]
        for g in range(1, tok // 8):
            packed += pltpu.roll(index_rows[8 * g : 8 * g + 8], g * top, 1)
        parts = [xs[pl.ds(h, tok, stride=heads), :], packed]
        extra = msg.shape[1] - tok - 8
        if extra:
            parts.append(jnp.zeros((extra, feat), F32))
        both = jnp.concatenate(parts, axis=0)
        msg[h] = both.astype(BF16)
    pl.semaphore_wait(barrier, heads)

    def copy_a(peer, sender):
        return pltpu.make_async_remote_copy(
            src_ref=msg.at[peer],
            dst_ref=inbox.at[sender * shards + my_d],
            send_sem=send_a.at[peer],
            recv_sem=recv_a.at[sender * shards + my_d],
            device_id={"head": peer, "dp": my_d},
            device_id_type=MESH,
        )

    def forward(sender, side):
        slot = sender * shards + side
        return pltpu.make_async_remote_copy(
            src_ref=inbox.at[slot],
            dst_ref=inbox.at[slot],
            send_sem=send_f.at[sender],
            recv_sem=recv_a.at[slot],
            device_id={"head": my_h, "dp": 1 - my_d},
            device_id_type=MESH,
        )

    def send_rows(step, carry):
        copy_a(lax.rem(my_h + step, heads), my_h).start()
        return carry

    lax.fori_loop(1, heads, send_rows, 0)
    inbox[me] = msg[my_h]
    forward(my_h, my_d).start()

    load_b.wait()
    load_v.wait()
    whole = bias[...]
    high = whole.astype(BF16).astype(F32)
    mid = (whole - high).astype(BF16).astype(F32)
    low = whole - high - mid
    stacked = jnp.concatenate([high, mid, low, jnp.zeros((5, share), F32)], axis=0)
    wide[:, pl.ds(feat, feat)] = jnp.zeros((share, feat), BF16)
    wide[:, pl.ds(feat, 8)] = jnp.transpose(stacked).astype(BF16)
    load_d.wait()
    for b in range(blocks):
        dec_t[b] = jnp.transpose(dec[pl.ds(b * stride, stride), :])
    load_w.wait()

    def take_rows(step, carry):
        source = lax.rem(my_h - step + heads, heads)
        copy_a(source, source).wait_recv()
        forward(source, my_d).start()
        return carry

    lax.fori_loop(1, heads, take_rows, 0)

    def take_forwarded(step, carry):
        forward(lax.rem(my_h - step + heads, heads), 1 - my_d).wait_recv()
        return carry

    lax.fori_loop(0, heads, take_forwarded, 0)

    arrived = inbox[...].astype(F32)
    x = arrived[:, 0:tok, :].reshape(rows, feat)
    packed_rows = arrived[:, tok : tok + 8, :].reshape(peers * 8, feat)
    groups = [
        (pltpu.roll(packed_rows, feat - g * top, 1) if g else packed_rows).reshape(peers, 8, feat)
        for g in range(tok // 8)
    ]
    index_t = jnp.transpose(jnp.concatenate(groups, axis=1).reshape(rows, feat))[0:top, :]
    size_t = jnp.abs(index_t)
    squares = jnp.sum(jnp.sum(x * x, axis=0, keepdims=True), axis=1, keepdims=True)
    scale = lax.rsqrt(squares / (rows * feat) + EPSILON)
    normed = x * scale
    vec = decb_ref[...]
    encoder_in = (normed - vec).astype(BF16)
    ones = (lax.broadcasted_iota(jnp.int32, (rows, feat), 1) < 3).astype(F32).astype(BF16)
    joint = jnp.concatenate([encoder_in, ones], axis=1)

    wanted = lax.broadcasted_iota(jnp.int32, (blocks, rows), 0) + my_d * blocks
    one = jnp.ones_like(wanted)
    unit = (one << (wanted & 15)).astype(F32) * jnp.where(wanted >= 16, 65536.0, 1.0)
    inverse = (one << (15 - (wanted & 15))).astype(F32) * (
        jnp.where(wanted >= 16, 2.0**-31, 2.0**-15)
    )
    least, limit = unit * half, unit * stride
    found = jnp.zeros((blocks, rows), F32)
    for k in range(top):
        size = size_t[k : k + 1, :]
        found = jnp.where((size >= least) & (size < limit), index_t[k : k + 1, :], found)
    offset = jnp.abs(found) * inverse - jnp.where(found < 0, 0.0, float(half))
    offs[...] = offset.astype(jnp.int32)

    latent = lax.broadcasted_iota(jnp.int32, (stride, rows), 0)

    def encode(b, carry):
        here = pl.ds(pl.multiple_of(b * stride, stride), stride)
        scores = lax.dot_general(
            wide[here, :], joint, (((1,), (1,)), ((), ())), preferred_element_type=F32
        )
        block = jnp.where(latent == offs[pl.ds(b, 1), :], scores, 0.0).astype(BF16)
        codes[here, :] = block
        return carry

    lax.fori_loop(0, blocks, encode, 0, unroll=8)
    total = jnp.dot(dec_t[0], codes[0:stride, :], preferred_element_type=F32)
    for b in range(1, blocks):
        here = pl.ds(b * stride, stride)
        total += jnp.dot(dec_t[b], codes[here, :], preferred_element_type=F32)
    acc[...] = total

    partner = pltpu.make_async_remote_copy(
        src_ref=acc, dst_ref=acc_in, send_sem=send_b, recv_sem=recv_b,
        device_id={"head": my_h, "dp": 1 - my_d}, device_id_type=MESH,
    )
    partner.start()
    center = jnp.sum(x, axis=0, keepdims=True) * scale / rows
    spread = jnp.sum(jnp.square(normed - center))
    partner.wait_recv()

    recon_normed = jnp.transpose(acc[...] + acc_in[...]) + vec
    rebuilt[...] = recon_normed / scale
    for h in range(heads):
        start = pl.multiple_of((h * shards + my_d) * tok, 8)
        part = rebuilt[pl.ds(start, tok), :]
        extra = reply.shape[1] - tok
        if extra:
            part = jnp.concatenate([part, jnp.zeros((extra, feat), F32)], axis=0)
        reply[h] = part.astype(BF16)

    def copy_c(peer, slot):
        return pltpu.make_async_remote_copy(
            src_ref=reply.at[peer],
            dst_ref=back.at[slot],
            send_sem=send_c.at[peer],
            recv_sem=recv_c.at[slot],
            device_id={"head": peer, "dp": my_d},
            device_id_type=MESH,
        )

    def send_back(step, carry):
        copy_c(lax.rem(my_h + step, heads), my_h).start()
        return carry

    lax.fori_loop(1, heads, send_back, 0)
    back[my_h] = reply[my_h]

    mismatch = recon_normed - normed
    error = (mismatch * (latents / (rows * top))).astype(BF16)
    expl_ref[0] = 1.0 - jnp.sum(mismatch * mismatch) / spread

    def gradient(b, carry):
        here = pl.ds(pl.multiple_of(b * stride, stride), stride)
        grad_ref[0, here, :] = jnp.dot(codes[here, :], error, preferred_element_type=F32)
        return carry

    lax.fori_loop(0, blocks, gradient, 0, unroll=4)

    def take_back(step, carry):
        source = lax.rem(my_h - step + heads, heads)
        copy_c(source, source).wait_recv()
        return carry

    lax.fori_loop(1, heads, take_back, 0)
    for h in range(heads):
        result[pl.ds(h, tok, stride=heads), :] = back[h].astype(F32)[0:tok, :]
    recon_ref[...] = result[...].reshape(tok, heads, feat).astype(BF16)

    partner.wait_send()

    def sent_a(step, carry):
        peer = lax.rem(my_h + step, heads)
        copy_a(peer, my_h).wait_send()
        forward(peer, my_d).wait_send()
        return carry

    lax.fori_loop(1, heads, sent_a, 0)
    forward(my_h, my_d).wait_send()

    def sent_c(step, carry):
        copy_c(lax.rem(my_h + step, heads), my_h).wait_send()
        return carry

    lax.fori_loop(1, heads, sent_c, 0)


def store_kernel(recon_in, expl_in, grad_in, recon_ref, expl_ref, grad_ref, sems):
    size = grad_in.shape[1] // PARTS
    copies = [pltpu.make_async_copy(recon_in, recon_ref, sems.at[PARTS])]
    for part in range(PARTS):
        here = pl.ds(part * size, size)
        copies.append(
            pltpu.make_async_copy(grad_in.at[:, here, :], grad_ref.at[:, here, :], sems.at[part])
        )
    for copy in copies:
        copy.start()
    expl_ref[0] = expl_in[0]
    for copy in copies:
        copy.wait()


def per_device(heads, shards, head_outputs, active, enc_weight, enc_bias, dec_weight, dec_bias):
    tok, _, feat = head_outputs.shape
    latents = enc_weight.shape[1]
    top = active.shape[2]
    share = latents // shards
    stride = latents // top
    blocks = share // stride
    peers = heads * shards
    rows = peers * tok
    back_rows = round_up(tok, PAD)
    msg_rows = round_up(tok + 8, PAD)
    vmem = pl.BlockSpec(memory_space=pltpu.VMEM)
    hbm = pl.BlockSpec(memory_space=pltpu.HBM)
    results = pl.pallas_call(
        functools.partial(step_kernel, heads, shards),
        out_shape=(
            jax.ShapeDtypeStruct((tok, heads, feat), BF16),
            jax.ShapeDtypeStruct((1,), F32),
            jax.ShapeDtypeStruct((1, share, feat), F32),
        ),
        in_specs=[hbm] * 6,
        out_specs=(vmem, pl.BlockSpec(memory_space=pltpu.SMEM), vmem),
        scratch_shapes=[
            pltpu.VMEM((tok, heads, feat), BF16),
            pltpu.VMEM((tok, heads, top), jnp.int32),
            pltpu.VMEM((1, feat), F32),
            pltpu.VMEM((tok * heads, feat), F32),
            pltpu.VMEM((tok * heads, feat), F32),
            pltpu.VMEM((heads, msg_rows, feat), BF16),
            pltpu.VMEM((peers, msg_rows, feat), BF16),
            pltpu.VMEM((share, 2 * feat), BF16),
            pltpu.VMEM((share, feat), BF16),
            pltpu.VMEM((blocks, feat, stride), BF16),
            pltpu.VMEM((1, share), F32),
            pltpu.VMEM((share, rows), BF16),
            pltpu.VMEM((blocks, rows), jnp.int32),
            pltpu.VMEM((feat, rows), F32),
            pltpu.VMEM((feat, rows), F32),
            pltpu.VMEM((rows, feat), F32),
            pltpu.VMEM((heads, back_rows, feat), BF16),
            pltpu.VMEM((heads, back_rows, feat), BF16),
            pltpu.VMEM((tok * heads, feat), F32),
            pltpu.SemaphoreType.DMA((6,)),
            pltpu.SemaphoreType.DMA((heads,)),
            pltpu.SemaphoreType.DMA((peers,)),
            pltpu.SemaphoreType.DMA((heads,)),
            pltpu.SemaphoreType.DMA,
            pltpu.SemaphoreType.DMA,
            pltpu.SemaphoreType.DMA((heads,)),
            pltpu.SemaphoreType.DMA((heads,)),
        ],
        compiler_params=pltpu.CompilerParams(
            collective_id=0, has_side_effects=True, vmem_limit_bytes=48 * 1024 * 1024
        ),
    )(*(
        pltpu.with_memory_space_constraint(operand, pltpu.HBM)
        for operand in (head_outputs, active, enc_weight, enc_bias, dec_weight, dec_bias)
    ))
    smem = pl.BlockSpec(memory_space=pltpu.SMEM)
    return pl.pallas_call(
        store_kernel,
        out_shape=tuple(jax.ShapeDtypeStruct(r.shape, r.dtype) for r in results),
        in_specs=[vmem, smem, vmem],
        out_specs=(hbm, smem, hbm),
        scratch_shapes=[pltpu.SemaphoreType.DMA((1 + PARTS,))],
        compiler_params=pltpu.CompilerParams(vmem_limit_bytes=16 * 1024 * 1024),
    )(*results)


def solution(mesh):
    placed = (
        P(("groups", "head", "dp"), None, None),
        P(("groups", "head", "dp"), None, None),
        P(("groups", "head"), None, None),
        P(("groups", "head"), None),
        P(("groups", "head"), None, None),
        P(("groups", "head"), None),
    )
    return jax.shard_map(
        functools.partial(per_device, mesh.shape["head"], mesh.shape["dp"]),
        mesh=mesh,
        in_specs=placed,
        out_specs=(
            P(("groups", "head", "dp"), None, None),
            P(("groups", "head")),
            P(("groups", "head"), "dp", None),
        ),
        check_vma=False,
    )
```

```python
import functools

import jax
import jax.numpy as jnp
from jax import lax
from jax.experimental import pallas as pl
from jax.experimental.pallas import tpu as pltpu
from jax.sharding import PartitionSpec as P

EPSILON = 1e-06
F32 = jnp.float32
BF16 = jnp.bfloat16
MESH = pl.DeviceIdType.MESH
PAD = 16
PARTS = 4
CUTS = 4


def round_up(value, unit):
    return (value + unit - 1) // unit * unit


def step_kernel(
    heads, shards, x_hbm, act_hbm, encw_ref, encb_ref, decw_ref, decb_hbm,
    recon_ref, expl_ref, grad_ref,
    x_ref, act_ref, decb_ref, xs, acts, msg, inbox, wide, dec, dec_t, bias, codes, offs, acc, acc_in, rebuilt, reply, back, result,
    local_sem, send_a, recv_a, send_f, send_b, recv_b, send_c, recv_c,
):
    tok = x_ref.shape[0]
    feat = x_ref.shape[2]
    top = act_ref.shape[2]
    latents = encw_ref.shape[1]
    share = latents // shards
    stride = latents // top
    shift = stride.bit_length() - 1
    blocks = share // stride
    peers = heads * shards
    rows = peers * tok
    my_h = lax.axis_index("head")
    my_d = lax.axis_index("dp")
    me = my_h * shards + my_d

    first = pl.multiple_of(my_d * share, share)
    load_w = pltpu.make_async_copy(
        encw_ref.at[0, pl.ds(first, share), :], wide.at[:, pl.ds(0, feat)], local_sem.at[0]
    )
    load_d = pltpu.make_async_copy(decw_ref.at[0, pl.ds(first, share), :], dec, local_sem.at[1])
    load_b = pltpu.make_async_copy(encb_ref.at[:, pl.ds(first, share)], bias, local_sem.at[2])
    load_x = pltpu.make_async_copy(x_hbm, x_ref, local_sem.at[3])
    load_a = pltpu.make_async_copy(act_hbm, act_ref, local_sem.at[4])
    load_v = pltpu.make_async_copy(decb_hbm, decb_ref, local_sem.at[5])
    load_x.start()
    load_a.start()
    load_b.start()
    load_v.start()
    load_d.start()
    load_w.start()

    barrier = pltpu.get_barrier_semaphore()

    def greet(step, carry):
        pl.semaphore_signal(
            barrier, inc=1,
            device_id={"head": lax.rem(my_h + step, heads), "dp": my_d}, device_id_type=MESH,
        )
        return carry

    lax.fori_loop(1, heads, greet, 0)
    pl.semaphore_signal(
        barrier, inc=1, device_id={"head": my_h, "dp": 1 - my_d}, device_id_type=MESH
    )

    load_x.wait()
    load_a.wait()
    xs[...] = x_ref[...].astype(F32).reshape(tok * heads, feat)
    picked = act_ref[...].reshape(tok * heads, top)
    acts[...] = jnp.zeros_like(acts)
    half = stride // 2
    band = picked >> shift
    inner = ((picked & (half - 1)) + half) << (band & 15)
    code = inner.astype(F32) * jnp.where(band >= 16, 65536.0, 1.0)
    acts[:, 0:top] = jnp.where((picked & half) != 0, -code, code)
    for h in range(heads):
        index_rows = acts[pl.ds(h, tok, stride=heads), :]
        packed = index_rows[0:8]
        for g in range(1, tok // 8):
            packed += pltpu.roll(index_rows[8 * g : 8 * g + 8], g * top, 1)
        parts = [xs[pl.ds(h, tok, stride=heads), :], packed]
        extra = msg.shape[1] - tok - 8
        if extra:
            parts.append(jnp.zeros((extra, feat), F32))
        both = jnp.concatenate(parts, axis=0)
        msg[h] = both.astype(BF16)
    pl.semaphore_wait(barrier, heads)

    def copy_a(peer, sender):
        return pltpu.make_async_remote_copy(
            src_ref=msg.at[peer],
            dst_ref=inbox.at[sender * shards + my_d],
            send_sem=send_a.at[peer],
            recv_sem=recv_a.at[sender * shards + my_d],
            device_id={"head": peer, "dp": my_d},
            device_id_type=MESH,
        )

    def forward(sender, side):
        slot = sender * shards + side
        return pltpu.make_async_remote_copy(
            src_ref=inbox.at[slot],
            dst_ref=inbox.at[slot],
            send_sem=send_f.at[sender],
            recv_sem=recv_a.at[slot],
            device_id={"head": my_h, "dp": 1 - my_d},
            device_id_type=MESH,
        )

    def send_rows(step, carry):
        copy_a(lax.rem(my_h + step, heads), my_h).start()
        return carry

    lax.fori_loop(1, heads, send_rows, 0)
    inbox[me] = msg[my_h]
    forward(my_h, my_d).start()

    load_b.wait()
    load_v.wait()
    whole = bias[...]
    high = whole.astype(BF16).astype(F32)
    mid = (whole - high).astype(BF16).astype(F32)
    low = whole - high - mid
    stacked = jnp.concatenate([high, mid, low, jnp.zeros((5, share), F32)], axis=0)
    wide[:, pl.ds(feat, feat)] = jnp.zeros((share, feat), BF16)
    wide[:, pl.ds(feat, 8)] = jnp.transpose(stacked).astype(BF16)
    load_d.wait()
    for b in range(blocks):
        dec_t[:, pl.ds(b * stride, stride)] = jnp.transpose(dec[pl.ds(b * stride, stride), :])
    load_w.wait()

    def take_rows(step, carry):
        source = lax.rem(my_h - step + heads, heads)
        copy_a(source, source).wait_recv()
        forward(source, my_d).start()
        return carry

    lax.fori_loop(1, heads, take_rows, 0)

    def take_forwarded(step, carry):
        forward(lax.rem(my_h - step + heads, heads), 1 - my_d).wait_recv()
        return carry

    lax.fori_loop(0, heads, take_forwarded, 0)

    arrived = inbox[...].astype(F32)
    x = arrived[:, 0:tok, :].reshape(rows, feat)
    packed_rows = arrived[:, tok : tok + 8, :].reshape(peers * 8, feat)
    groups = [
        (pltpu.roll(packed_rows, feat - g * top, 1) if g else packed_rows).reshape(peers, 8, feat)
        for g in range(tok // 8)
    ]
    index_t = jnp.transpose(jnp.concatenate(groups, axis=1).reshape(rows, feat))[0:top, :]
    size_t = jnp.abs(index_t)
    squares = jnp.sum(jnp.sum(x * x, axis=0, keepdims=True), axis=1, keepdims=True)
    scale = lax.rsqrt(squares / (rows * feat) + EPSILON)
    normed = x * scale
    vec = decb_ref[...]
    encoder_in = (normed - vec).astype(BF16)
    ones = (lax.broadcasted_iota(jnp.int32, (rows, feat), 1) < 3).astype(F32).astype(BF16)
    joint = jnp.concatenate([encoder_in, ones], axis=1)

    wanted = lax.broadcasted_iota(jnp.int32, (blocks, rows), 0) + my_d * blocks
    one = jnp.ones_like(wanted)
    unit = (one << (wanted & 15)).astype(F32) * jnp.where(wanted >= 16, 65536.0, 1.0)
    inverse = (one << (15 - (wanted & 15))).astype(F32) * (
        jnp.where(wanted >= 16, 2.0**-31, 2.0**-15)
    )
    least, limit = unit * half, unit * stride
    found = jnp.zeros((blocks, rows), F32)
    for k in range(top):
        size = size_t[k : k + 1, :]
        found = jnp.where((size >= least) & (size < limit), index_t[k : k + 1, :], found)
    offset = jnp.abs(found) * inverse - jnp.where(found < 0, 0.0, float(half))
    offs[...] = offset.astype(jnp.int32)

    latent = lax.broadcasted_iota(jnp.int32, (stride, rows), 0)

    def encode(b, carry):
        here = pl.ds(pl.multiple_of(b * stride, stride), stride)
        scores = lax.dot_general(
            wide[here, :], joint, (((1,), (1,)), ((), ())), preferred_element_type=F32
        )
        block = jnp.where(latent == offs[pl.ds(b, 1), :], scores, 0.0).astype(BF16)
        codes[here, :] = block
        return carry

    lax.fori_loop(0, blocks, encode, 0, unroll=8)
    acc[...] = jnp.dot(dec_t[...], codes[...], preferred_element_type=F32)

    partner = []
    for part in range(CUTS):
        here = pl.ds(part * (feat // CUTS), feat // CUTS)
        partner.append(
            pltpu.make_async_remote_copy(
                src_ref=acc.at[here, :], dst_ref=acc_in.at[here, :],
                send_sem=send_b.at[part], recv_sem=recv_b.at[part],
                device_id={"head": my_h, "dp": 1 - my_d}, device_id_type=MESH,
            )
        )
    for copy in partner:
        copy.start()
    center = jnp.sum(x, axis=0, keepdims=True) * scale / rows
    spread = jnp.sum(jnp.square(normed - center))
    for copy in partner:
        copy.wait_recv()

    recon_normed = jnp.transpose(acc[...] + acc_in[...]) + vec
    rebuilt[...] = recon_normed / scale
    for h in range(heads):
        start = pl.multiple_of((h * shards + my_d) * tok, 8)
        part = rebuilt[pl.ds(start, tok), :]
        extra = reply.shape[1] - tok
        if extra:
            part = jnp.concatenate([part, jnp.zeros((extra, feat), F32)], axis=0)
        reply[h] = part.astype(BF16)

    def copy_c(peer, slot):
        return pltpu.make_async_remote_copy(
            src_ref=reply.at[peer],
            dst_ref=back.at[slot],
            send_sem=send_c.at[peer],
            recv_sem=recv_c.at[slot],
            device_id={"head": peer, "dp": my_d},
            device_id_type=MESH,
        )

    def send_back(step, carry):
        copy_c(lax.rem(my_h + step, heads), my_h).start()
        return carry

    lax.fori_loop(1, heads, send_back, 0)
    back[my_h] = reply[my_h]

    mismatch = recon_normed - normed
    error = (mismatch * (latents / (rows * top))).astype(BF16)
    expl_ref[0] = 1.0 - jnp.sum(mismatch * mismatch) / spread

    def gradient(b, carry):
        here = pl.ds(pl.multiple_of(b * stride, stride), stride)
        grad_ref[0, here, :] = jnp.dot(codes[here, :], error, preferred_element_type=F32)
        return carry

    lax.fori_loop(0, blocks, gradient, 0, unroll=4)

    def take_back(step, carry):
        source = lax.rem(my_h - step + heads, heads)
        copy_c(source, source).wait_recv()
        return carry

    lax.fori_loop(1, heads, take_back, 0)
    for h in range(heads):
        result[pl.ds(h, tok, stride=heads), :] = back[h].astype(F32)[0:tok, :]
    recon_ref[...] = result[...].reshape(tok, heads, feat).astype(BF16)

    for copy in partner:
        copy.wait_send()

    def sent_a(step, carry):
        peer = lax.rem(my_h + step, heads)
        copy_a(peer, my_h).wait_send()
        forward(peer, my_d).wait_send()
        return carry

    lax.fori_loop(1, heads, sent_a, 0)
    forward(my_h, my_d).wait_send()

    def sent_c(step, carry):
        copy_c(lax.rem(my_h + step, heads), my_h).wait_send()
        return carry

    lax.fori_loop(1, heads, sent_c, 0)


def store_kernel(recon_in, expl_in, grad_in, recon_ref, expl_ref, grad_ref, sems):
    size = grad_in.shape[1] // PARTS
    copies = [pltpu.make_async_copy(recon_in, recon_ref, sems.at[PARTS])]
    for part in range(PARTS):
        here = pl.ds(part * size, size)
        copies.append(
            pltpu.make_async_copy(grad_in.at[:, here, :], grad_ref.at[:, here, :], sems.at[part])
        )
    for copy in copies:
        copy.start()
    expl_ref[0] = expl_in[0]
    for copy in copies:
        copy.wait()


def per_device(heads, shards, head_outputs, active, enc_weight, enc_bias, dec_weight, dec_bias):
    tok, _, feat = head_outputs.shape
    latents = enc_weight.shape[1]
    top = active.shape[2]
    share = latents // shards
    stride = latents // top
    blocks = share // stride
    peers = heads * shards
    rows = peers * tok
    back_rows = round_up(tok, PAD)
    msg_rows = round_up(tok + 8, PAD)
    vmem = pl.BlockSpec(memory_space=pltpu.VMEM)
    hbm = pl.BlockSpec(memory_space=pltpu.HBM)
    results = pl.pallas_call(
        functools.partial(step_kernel, heads, shards),
        out_shape=(
            jax.ShapeDtypeStruct((tok, heads, feat), BF16),
            jax.ShapeDtypeStruct((1,), F32),
            jax.ShapeDtypeStruct((1, share, feat), F32),
        ),
        in_specs=[hbm] * 6,
        out_specs=(vmem, pl.BlockSpec(memory_space=pltpu.SMEM), vmem),
        scratch_shapes=[
            pltpu.VMEM((tok, heads, feat), BF16),
            pltpu.VMEM((tok, heads, top), jnp.int32),
            pltpu.VMEM((1, feat), F32),
            pltpu.VMEM((tok * heads, feat), F32),
            pltpu.VMEM((tok * heads, feat), F32),
            pltpu.VMEM((heads, msg_rows, feat), BF16),
            pltpu.VMEM((peers, msg_rows, feat), BF16),
            pltpu.VMEM((share, 2 * feat), BF16),
            pltpu.VMEM((share, feat), BF16),
            pltpu.VMEM((feat, share), BF16),
            pltpu.VMEM((1, share), F32),
            pltpu.VMEM((share, rows), BF16),
            pltpu.VMEM((blocks, rows), jnp.int32),
            pltpu.VMEM((feat, rows), F32),
            pltpu.VMEM((feat, rows), F32),
            pltpu.VMEM((rows, feat), F32),
            pltpu.VMEM((heads, back_rows, feat), BF16),
            pltpu.VMEM((heads, back_rows, feat), BF16),
            pltpu.VMEM((tok * heads, feat), F32),
            pltpu.SemaphoreType.DMA((6,)),
            pltpu.SemaphoreType.DMA((heads,)),
            pltpu.SemaphoreType.DMA((peers,)),
            pltpu.SemaphoreType.DMA((heads,)),
            pltpu.SemaphoreType.DMA((CUTS,)),
            pltpu.SemaphoreType.DMA((CUTS,)),
            pltpu.SemaphoreType.DMA((heads,)),
            pltpu.SemaphoreType.DMA((heads,)),
        ],
        compiler_params=pltpu.CompilerParams(
            collective_id=0, has_side_effects=True, vmem_limit_bytes=48 * 1024 * 1024
        ),
    )(*(
        pltpu.with_memory_space_constraint(operand, pltpu.HBM)
        for operand in (head_outputs, active, enc_weight, enc_bias, dec_weight, dec_bias)
    ))
    smem = pl.BlockSpec(memory_space=pltpu.SMEM)
    return pl.pallas_call(
        store_kernel,
        out_shape=tuple(jax.ShapeDtypeStruct(r.shape, r.dtype) for r in results),
        in_specs=[vmem, smem, vmem],
        out_specs=(hbm, smem, hbm),
        scratch_shapes=[pltpu.SemaphoreType.DMA((1 + PARTS,))],
        compiler_params=pltpu.CompilerParams(vmem_limit_bytes=16 * 1024 * 1024),
    )(*results)


def solution(mesh):
    placed = (
        P(("groups", "head", "dp"), None, None),
        P(("groups", "head", "dp"), None, None),
        P(("groups", "head"), None, None),
        P(("groups", "head"), None),
        P(("groups", "head"), None, None),
        P(("groups", "head"), None),
    )
    return jax.shard_map(
        functools.partial(per_device, mesh.shape["head"], mesh.shape["dp"]),
        mesh=mesh,
        in_specs=placed,
        out_specs=(
            P(("groups", "head", "dp"), None, None),
            P(("groups", "head")),
            P(("groups", "head"), "dp", None),
        ),
        check_vma=False,
    )
```
